128 devices in a mesh: dp: 16 (over z, y), pipe: 2 (over x_hi), tensor: 4 (over x_lo, core).
Axes of the slice: x: 4 (x_hi: 2, x_lo: 2; x = x_hi * 2 + x_lo), y: 4, z: 4, core: 2. Of those that a mesh axis runs over, the one named last changes fastest.
Arguments:
- residual_input: bfloat16 [1024, 8192], P('dp', 'tensor'), may hold values from -6 to 6
- layer_norm_gain: bfloat16 [2, 8192], P('pipe'), may hold values from 0.099609375 to 1.8984375
- query_weight: bfloat16 [2, 8192, 8192], P('pipe', 'dp', 'tensor'), may hold values from -0.0625 to 0.0625
- key_weight: bfloat16 [2, 8192, 1024], P('pipe', 'dp', 'tensor'), may hold values from -0.0625 to 0.0625
- value_weight: bfloat16 [2, 8192, 1024], P('pipe', 'dp', 'tensor'), may hold values from -0.0625 to 0.0625
- output_weight: bfloat16 [2, 8192, 8192], P('pipe', 'tensor', 'dp'), may hold values from -0.0625 to 0.0625
- adapter_down_weight: bfloat16 [2, 8192, 8, 128], P('pipe', 'tensor'), may hold values from -0.0625 to 0.0625
- adapter_up_weight: bfloat16 [2, 8, 128, 8192], P('pipe', None, None, 'tensor'), may hold values from -0.5 to 0.5
- cached_key_rows: bfloat16 [2, 1024, 80, 1024], P('pipe', 'dp', None, 'tensor'), may hold values from -280 to 280
- cached_value_rows: bfloat16 [2, 1024, 80, 1024], P('pipe', 'dp', None, 'tensor'), may hold values from -6 to 6
- request_adapter: int32 [1024], P('dp'), may hold values from 0 to 7
- rank_per_adapter: int32 [8], replicated, may hold values from 16 to 128, as said below
- cached_length: int32 [1024], P('dp'), may hold values from 1 to 80, as said below
Outputs:
- hidden_out: bfloat16 [1024, 8192], P(('dp', 'pipe'), 'tensor')
The draws below stay inside these ranges and needn't reach their ends.
Inputs may be any that keep to these rules, and one draw needn't show every extreme that they name: `rank_per_adapter`: some adapter has rank exactly 128. `cached_length`: some request has exactly 80 cached positions; a request's new token stands at the position equal to its length.
All inputs are finite; a program needn't handle non-finite values.
Results may differ from the reference program's by a relative error of at most 0.025.
Values may be sent and summed in bfloat16 or wider, within the bound.
No kernel may reach another device: no remote copies, remote signals or barrier semaphores. Data moves between devices by JAX's collectives and lax.ppermute only.
A program may use at most 128 MiB of HBM per device.

```python
import math
import jax
import jax.numpy as jnp
import numpy as np
from jax import lax

MODEL_WIDTH = 8192
QUERY_HEADS = 64
KV_HEADS = 8
HEAD_SIZE = 128
ADAPTER_RANK = 128
ADAPTER_COUNT = 8
CTX = 80
QUERY_FEATURES = 8192
KVD = 1024
LAYER_COUNT = 2
REQUESTS = 1024


def draw_cached_key_rows(key, part):
    key = jax.random.fold_in(key, 11)
    base_draw = jnp.clip(jax.random.normal(key, (LAYER_COUNT, REQUESTS, CTX, KVD), jnp.float32), -6.0, 6.0)
    return base_draw.astype(jnp.bfloat16)


def draw_rank_per_adapter(key, part):
    key = jax.random.fold_in(key, 5)
    ranks_drawn = jax.random.randint(key, (ADAPTER_COUNT,), ADAPTER_RANK // 8, ADAPTER_RANK + 1, dtype=jnp.int32)
    chosen = jax.random.randint(jax.random.fold_in(key, 1), (), 0, ADAPTER_COUNT, dtype=jnp.int32)
    return jnp.where(jnp.arange(ADAPTER_COUNT, dtype=jnp.int32) == chosen, ADAPTER_RANK, ranks_drawn).astype(jnp.int32)


def draw_cached_length(key, part):
    key = jax.random.fold_in(key, 7)
    lengths_drawn = jax.random.randint(key, (REQUESTS,), 1, CTX + 1, dtype=jnp.int32)
    chosen = jax.random.randint(jax.random.fold_in(key, 1), (), 0, REQUESTS, dtype=jnp.int32)
    return jnp.where(jnp.arange(REQUESTS, dtype=jnp.int32) == chosen, CTX, lengths_drawn).astype(jnp.int32)


def with_ends(result, own_key, least, largest):
    spot = [jax.random.randint(jax.random.fold_in(own_key, axis), (), 0, length) for axis, length in enumerate(result.shape)]
    widest = result.shape.index(max(result.shape))
    next_to = spot[:widest] + [(spot[widest] + 1) % result.shape[widest]] + spot[widest + 1:]
    return result.at[tuple(spot)].set(least).at[tuple(next_to)].set(largest)


def shard_levels(stream_key, shape, cuts, least, top_value):
    loudness, own = 1.0, jax.random.fold_in(stream_key, 6)
    for axis_at, shards_of in cuts:
        draws = jnp.exp(jax.random.uniform(jax.random.fold_in(own, axis_at), (shards_of,), jnp.float32, least / len(cuts), top_value / len(cuts)))
        loudness = loudness * jnp.repeat(draws, shape[axis_at] // shards_of).reshape([-1 if axis == axis_at else 1 for axis in range(len(shape))])
    return loudness


def rank_bounds(count, lean):
    portions = [(1 << 20) // math.isqrt(standing ** lean) + 1 for standing in range(1, count + 1)]
    scale = 1 + sum(portions) // (1 << 30)
    return np.cumsum(np.array([max(1, weight // scale) for weight in portions]))


def ranked(own_key, shape, number_of, skew):
    table = rank_bounds(number_of, skew)
    lot = jax.random.randint(jax.random.fold_in(own_key, 1), shape, 0, int(table[number_of - 1]))
    standing = jnp.searchsorted(jnp.asarray(table, jnp.int32), lot, side="right")
    return jax.random.permutation(jax.random.fold_in(own_key, 2), number_of)[standing].astype(jnp.int32)


def bell_draw(stream_key, dims, width, bound, shards=(), held_as=jnp.bfloat16):
    result = width * jax.random.normal(stream_key, dims, jnp.float32)
    if shards:
        result = result * shard_levels(stream_key, dims, shards, -0.22, 0.18)
    return jnp.clip(result, -bound, bound).astype(held_as)


def setup_inputs(seed: int = 0) -> dict:
    seeds = jax.random.split(jax.random.key(seed), 14)
    return {
        "residual_input": bell_draw(seeds[0], (REQUESTS, MODEL_WIDTH), 1.0, 6.0, ((0, 16), (1, 4))),
        "layer_norm_gain": jnp.clip(1.0 + 0.18 * jax.random.normal(seeds[1], (LAYER_COUNT, MODEL_WIDTH), jnp.float32), 0.099609375, 1.8984375).astype(jnp.bfloat16),
        "query_weight": bell_draw(seeds[2], (LAYER_COUNT, MODEL_WIDTH, QUERY_FEATURES), MODEL_WIDTH ** -0.5, 0.0625, ((0, 2), (1, 16), (2, 4))),
        "key_weight": bell_draw(seeds[3], (LAYER_COUNT, MODEL_WIDTH, KVD), MODEL_WIDTH ** -0.5, 0.0625, ((0, 2), (1, 16), (2, 4))),
        "value_weight": bell_draw(seeds[4], (LAYER_COUNT, MODEL_WIDTH, KVD), MODEL_WIDTH ** -0.5, 0.0625, ((0, 2), (1, 16), (2, 4))),
        "output_weight": bell_draw(seeds[5], (LAYER_COUNT, QUERY_FEATURES, MODEL_WIDTH), QUERY_FEATURES ** -0.5, 0.0625, ((0, 2), (1, 4), (2, 16))),
        "adapter_down_weight": bell_draw(seeds[6], (LAYER_COUNT, QUERY_FEATURES, ADAPTER_COUNT, ADAPTER_RANK), QUERY_FEATURES ** -0.5, 0.0625, ((0, 2), (1, 4))),
        "adapter_up_weight": bell_draw(seeds[7], (LAYER_COUNT, ADAPTER_COUNT, ADAPTER_RANK, MODEL_WIDTH), ADAPTER_RANK ** -0.5, 0.5, ((0, 2), (3, 4))),
        "cached_key_rows": draw_cached_key_rows(jax.random.fold_in(seeds[13], 71), 0),
        "cached_value_rows": bell_draw(seeds[9], (LAYER_COUNT, REQUESTS, CTX, KVD), 1.0, 6.0, ((0, 2), (1, 16), (3, 4))),
        "request_adapter": with_ends(ranked(seeds[10], (REQUESTS,), ADAPTER_COUNT, 2), jax.random.fold_in(seeds[10], 3), 0, ADAPTER_COUNT - 1).astype(jnp.int32),
        "rank_per_adapter": draw_rank_per_adapter(jax.random.fold_in(seeds[13], 71), 0),
        "cached_length": draw_cached_length(jax.random.fold_in(seeds[13], 71), 0),
    }


epsilon = 1e-05
adapter_scale = 64.0

def rope_tables(positions, head_width):
    half_width = head_width // 2
    inv_freq = jnp.exp(-jnp.log(10000.0) * jnp.arange(half_width, dtype=jnp.float32) * (2.0 / head_width))
    angles = positions.astype(jnp.float32)[:, None] * inv_freq[None, :]
    return (jnp.cos(angles), jnp.sin(angles))

def rotate(features, cosine, sine_table):
    half_width = features.shape[-1] // 2
    first_half = features[..., :half_width]
    second_half = features[..., half_width:]
    return jnp.concatenate([first_half * cosine - second_half * sine_table, second_half * cosine + first_half * sine_table], axis=-1)

def apply_layer(residual_state, inverse_norm, query_weight, key_weight, value_weight, output_weight, adapter_down_weight, adapter_up_weight, layer_key_block, layer_value_block, request_adapter, rank_per_adapter, cached_length):
    request_count = residual_state.shape[0]
    residual_final = residual_state.astype(jnp.float32)
    norm_factor = lax.rsqrt(lax.optimization_barrier(jnp.mean(residual_final * residual_final, axis=-1, keepdims=True)) + epsilon)
    normed = (residual_final * norm_factor * inverse_norm.astype(jnp.float32)[None, :]).astype(jnp.bfloat16)
    query_raw = jnp.dot(normed, query_weight, preferred_element_type=jnp.float32)
    key_raw = jnp.dot(normed, key_weight, preferred_element_type=jnp.float32)
    value_raw = jnp.dot(normed, value_weight, preferred_element_type=jnp.float32)
    cosine, sine_table = rope_tables(cached_length, HEAD_SIZE)
    cosine = cosine[:, None, :]
    sine_table = sine_table[:, None, :]
    query_rot = rotate(query_raw.reshape(request_count, QUERY_HEADS, HEAD_SIZE), cosine, sine_table).astype(jnp.bfloat16)
    key_new = rotate(key_raw.reshape(request_count, KV_HEADS, HEAD_SIZE), cosine, sine_table).astype(jnp.bfloat16)
    value_new = value_raw.reshape(request_count, KV_HEADS, HEAD_SIZE).astype(jnp.bfloat16)
    group_size = QUERY_HEADS // KV_HEADS
    inverse = float(HEAD_SIZE) ** (-0.5)
    query_four = query_rot.reshape(request_count, KV_HEADS, group_size, HEAD_SIZE).astype(jnp.float32)
    keys_four = layer_key_block.reshape(request_count, CTX, KV_HEADS, HEAD_SIZE).astype(jnp.float32)
    values_four = layer_value_block.reshape(request_count, CTX, KV_HEADS, HEAD_SIZE).astype(jnp.float32)
    scores = jnp.einsum('rgqd,rcgd->rgqc', query_four, keys_four) * inverse
    own_score = jnp.einsum('rgqd,rgd->rgq', query_four, key_new.astype(jnp.float32)) * inverse
    valid = jnp.arange(CTX, dtype=jnp.int32)[None, :] < cached_length[:, None]
    masked = jnp.where(valid[:, None, None, :], scores, -1e+30)
    row_top = jnp.maximum(lax.optimization_barrier(jnp.max(masked, axis=-1)), own_score)
    weights_raw = jnp.exp(masked - row_top[..., None])
    own_raw = jnp.exp(own_score - row_top)
    denominator = lax.optimization_barrier(jnp.sum(weights_raw, axis=-1)) + own_raw
    weights = (weights_raw / denominator[..., None]).astype(jnp.bfloat16)
    own_weight = (own_raw / denominator).astype(jnp.bfloat16)
    attention_output = jnp.einsum('rgqc,rcgd->rgqd', weights.astype(jnp.float32), values_four)
    attention_output = attention_output + own_weight.astype(jnp.float32)[..., None] * value_new.astype(jnp.float32)[:, :, None, :]
    attention_output = attention_output.reshape(request_count, QUERY_HEADS * HEAD_SIZE).astype(jnp.bfloat16)
    plain_projection = jnp.dot(attention_output, output_weight, preferred_element_type=jnp.float32)
    adapter_selector = jnp.arange(ADAPTER_COUNT, dtype=jnp.int32)[None, :] == request_adapter[:, None]
    request_rank = lax.optimization_barrier(jnp.sum(jnp.where(adapter_selector, rank_per_adapter[None, :], 0), axis=1))
    adapter_product = jnp.dot(attention_output, adapter_down_weight.reshape(QUERY_HEADS * HEAD_SIZE, ADAPTER_COUNT * ADAPTER_RANK), preferred_element_type=jnp.float32)
    adapter_product = adapter_product.reshape(request_count, ADAPTER_COUNT, ADAPTER_RANK)
    selected_rows = lax.optimization_barrier(jnp.sum(jnp.where(adapter_selector[:, :, None], adapter_product, 0.0), axis=1))
    live_rank = jnp.arange(ADAPTER_RANK, dtype=jnp.int32)[None, :] < request_rank[:, None]
    selected_rows = jnp.where(live_rank, selected_rows, 0.0)
    reduced_rows = (selected_rows * (adapter_scale / request_rank.astype(jnp.float32))[:, None]).astype(jnp.bfloat16)
    layer_blocks = jnp.where(adapter_selector[:, :, None], reduced_rows[:, None, :], jnp.zeros((), jnp.bfloat16)).reshape(request_count, ADAPTER_COUNT * ADAPTER_RANK)
    adapter_update = jnp.dot(layer_blocks, adapter_up_weight.reshape(ADAPTER_COUNT * ADAPTER_RANK, MODEL_WIDTH), preferred_element_type=jnp.float32)
    return (residual_final + plain_projection + adapter_update).astype(jnp.bfloat16)

def reference(residual_input, layer_norm_gain, query_weight, key_weight, value_weight, output_weight, adapter_down_weight, adapter_up_weight, cached_key_rows, cached_value_rows, request_adapter, rank_per_adapter, cached_length):
    residual_state = residual_input
    for current_layer in range(LAYER_COUNT):
        residual_state = apply_layer(residual_state, layer_norm_gain[current_layer], query_weight[current_layer], key_weight[current_layer], value_weight[current_layer], output_weight[current_layer], adapter_down_weight[current_layer], adapter_up_weight[current_layer], cached_key_rows[current_layer], cached_value_rows[current_layer], request_adapter, rank_per_adapter, cached_length)
    return residual_state
```

```python
import jax
import jax.numpy as jnp
from jax import lax
from jax.sharding import PartitionSpec as P

HEAD = 128
RANK = 128
ADAPTERS = 8
CTX = 80
EPS = 1e-05
SCALE = 64.0
AXES = ("dp", "pipe", "tensor")
bf16 = jnp.bfloat16
f32 = jnp.float32


def send(block, route):
    pairs = []
    for z in range(4):
        for y in range(4):
            for p in range(2):
                for xl in range(2):
                    for c in range(2):
                        there = route(z, y, p, xl, c)
                        if there is None:
                            continue
                        source = ((z * 4 + y) * 2 + p) * 4 + xl * 2 + c
                        a, b, q, u, v = there
                        target = (((a % 4) * 4 + b % 4) * 2 + q) * 4 + u * 2 + v
                        pairs.append((source, target))
    return lax.ppermute(block, AXES, pairs)


def along(axis, step):
    if axis == "z":
        return lambda z, y, p, u, c: (z + step, y, p, u, c)
    if axis == "y":
        return lambda z, y, p, u, c: (z, y + step, p, u, c)

    def ring(z, y, p, u, c):
        x = (2 * p + u + step) % 4
        return (z, y, x // 2, x % 2, c)

    return ring


def other_core(z, y, p, u, c):
    return (z, y, p, u, 1 - c)


def other_xl(z, y, p, u, c):
    return (z, y, p, 1 - u, c)


def other_pipe(z, y, p, u, c):
    return (z, y, 1 - p, u, c)


def pipe_from(source):
    return lambda z, y, p, u, c: (z, y, 1 - p, u, c) if p == source else None


def rope_tables(positions):
    half = HEAD // 2
    inv_freq = jnp.exp(-jnp.log(10000.0) * jnp.arange(half, dtype=f32) * (2.0 / HEAD))
    angles = positions.astype(f32)[:, None] * inv_freq[None, :]
    return (jnp.cos(angles), jnp.sin(angles))


def rotate(features, cosine, sine):
    half = HEAD // 2
    a = features[..., :half]
    b = features[..., half:]
    return jnp.concatenate([a * cosine - b * sine, b * cosine + a * sine], axis=-1)


def attend(query, key_new, value_new, keys, values, lengths):
    rows, groups = key_new.shape[:2]
    inverse = float(HEAD) ** (-0.5)
    query = query.reshape(rows, groups, -1, HEAD)
    keys = keys.reshape(rows, CTX, groups, HEAD)
    values = values.reshape(rows, CTX, groups, HEAD)
    scores = jnp.einsum("rgqd,rcgd->rgqc", query, keys, preferred_element_type=f32) * inverse
    own = jnp.einsum("rgqd,rgd->rgq", query, key_new, preferred_element_type=f32) * inverse
    valid = jnp.arange(CTX, dtype=jnp.int32)[None, :] < lengths[:, None]
    masked = jnp.where(valid[:, None, None, :], scores, -1e30)
    top = jnp.maximum(jnp.max(masked, axis=-1), own)
    raw = jnp.exp(masked - top[..., None])
    own_raw = jnp.exp(own - top)
    total = jnp.sum(raw, axis=-1) + own_raw
    weights = (raw / total[..., None]).astype(bf16)
    own_weight = (own_raw / total).astype(bf16)
    out = jnp.einsum("rgqc,rcgd->rgqd", weights, values, preferred_element_type=f32)
    out = out + own_weight.astype(f32)[..., None] * value_new.astype(f32)[:, :, None, :]
    return out.reshape(rows, -1).astype(bf16)


def add_up(blocks):
    total = blocks[0].astype(f32)
    for block in blocks[1:]:
        total = total + block.astype(f32)
    return total


def on_device(
    residual_input,
    layer_norm_gain,
    query_weight,
    key_weight,
    value_weight,
    output_weight,
    adapter_down_weight,
    adapter_up_weight,
    cached_key_rows,
    cached_value_rows,
    request_adapter,
    rank_per_adapter,
    cached_length,
):
    d = lax.axis_index("dp")
    p = lax.axis_index("pipe")
    t = lax.axis_index("tensor")
    z, y = d // 4, d % 4
    x, core = 2 * p + t // 2, t % 2
    group = residual_input.shape[0]
    half = group // 2
    block = query_weight.shape[1]
    qh = query_weight.shape[2] // 2
    kh = key_weight.shape[2] // 2

    gain = lax.dynamic_slice_in_dim(layer_norm_gain[0], d * block, block, 0).astype(f32)[:, None]

    def in_half(which):
        parts = [
            lax.dynamic_slice_in_dim(query_weight[0], which * qh, qh, 1),
            lax.dynamic_slice_in_dim(key_weight[0], which * kh, kh, 1),
            lax.dynamic_slice_in_dim(value_weight[0], which * kh, kh, 1),
        ]
        return (jnp.concatenate(parts, axis=1).astype(f32) * gain).astype(bf16)

    mine_in = in_half(p)
    theirs_in = in_half(1 - p)
    from_zero = send(theirs_in, pipe_from(0))
    from_one = send(theirs_in, pipe_from(1))
    w_in = [jnp.where(p == 0, mine_in, from_zero), jnp.where(p == 1, mine_in, from_one)]

    out_mine = lax.dynamic_slice_in_dim(output_weight[0], p * qh, qh, 0)
    out_theirs = lax.dynamic_slice_in_dim(output_weight[0], (1 - p) * qh, qh, 0)
    out_theirs = lax.optimization_barrier((out_theirs, from_zero, from_one))[0]
    out_got = send(out_theirs, other_pipe)
    w_out = [jnp.where(p == 0, out_mine, out_got), jnp.where(p == 1, out_mine, out_got)]

    down = adapter_down_weight[0].reshape(-1, ADAPTERS * RANK)
    up = adapter_up_weight[0].reshape(ADAPTERS * RANK, -1)
    up = lax.dynamic_slice_in_dim(up, y * block, block, 1)
    up = lax.optimization_barrier((up, from_zero, from_one))[0]
    up = send(up, lambda z, y, p, u, c: (2 * u + c, y, p, z // 2, z % 2))

    slots = jnp.arange(ADAPTERS, dtype=jnp.int32)

    def relative(whole):
        whole = whole.reshape((4, 4) + whole.shape[1:])
        whole = jnp.concatenate([whole, whole], axis=0)
        whole = lax.dynamic_slice_in_dim(whole, z, 4, 0)
        whole = jnp.concatenate([whole, whole], axis=1)
        return lax.dynamic_slice_in_dim(whole, y, 4, 1)

    everyone = relative(lax.all_gather(request_adapter, "dp", axis=0, tiled=False))
    rows_of = [
        everyone[:, :, :half].reshape(4, -1),
        everyone[:, :, half:].transpose(1, 0, 2).reshape(4, -1),
    ]

    chosen = request_adapter[:, None] == slots[None, :]
    rank = jnp.sum(jnp.where(chosen, rank_per_adapter[None, :], 0), axis=1)
    live = jnp.arange(RANK, dtype=jnp.int32)[None, :] < rank[:, None]
    rank_scale = SCALE / rank.astype(f32)
    cosine, sine = rope_tables(cached_length)
    cosine, sine = cosine[:, None, :], sine[:, None, :]

    split = residual_input.reshape(group, 4, block)
    got = [None] * 4
    for k in range(4):
        piece = lax.dynamic_index_in_dim(split, (y + k) % 4, 1, keepdims=False)
        got[(4 - k) % 4] = send(
            piece, lambda z, y, p, u, c, k=k: (2 * u + c, y + k, p, z // 2, z % 2)
        )
    quarter = jnp.stack(got)
    near = send(quarter, other_xl)
    pair = jnp.stack([jnp.where(t < 2, quarter, near), jnp.where(t < 2, near, quarter)])
    far = send(pair, other_core)
    even, odd = jnp.where(core == 0, pair, far), jnp.where(core == 0, far, pair)
    rows = jnp.stack([even[0], odd[0], even[1], odd[1]])
    rows = lax.dynamic_slice_in_dim(jnp.concatenate([rows, rows], axis=0), z, 4, 0)
    state = [
        rows[:, :, :half].reshape(4, 4 * half, block),
        rows[:, :, half:].transpose(1, 0, 2, 3).reshape(4, 4 * half, block),
    ]

    square = residual_input.astype(f32)
    square = jnp.sum(square * square, axis=1).reshape(1, group)
    square = square + send(square, other_xl)
    square = square + send(square, other_core)
    square = square.reshape(group)

    first, second = ("z", "y"), ("y", "z")

    for layer in range(2):
        summed = [None, None]
        for h in range(2):
            parts = [None] * 4
            for k in (2, 1, 3, 0):
                part = jnp.dot(
                    state[h][k], w_in[layer], preferred_element_type=f32
                ).astype(bf16)
                parts[k] = part if k == 0 else send(part, along(first[h], k))
            summed[h] = add_up(parts).astype(bf16).reshape(4, half, -1)
        if layer == 1:
            squares = [jnp.sum(s.astype(f32) ** 2, axis=2).reshape(4, 4, half) for s in state]
            squares = jnp.concatenate([squares[0], squares[1].transpose(1, 0, 2)], axis=2)
            squares = jnp.concatenate([squares, squares], axis=0)
            squares = lax.dynamic_slice_in_dim(squares, (4 - z) % 4, 4, 0)
            squares = jnp.concatenate([squares, squares], axis=1)
            squares = lax.dynamic_slice_in_dim(squares, (4 - y) % 4, 4, 1)
            squares = lax.psum(squares.reshape(16, group), "dp")
            square = lax.dynamic_index_in_dim(squares, d, 0, keepdims=False)
        ours = [None, None]
        for h in range(2):
            parts = [summed[h][0]]
            for k in (2, 1, 3):
                parts.append(send(summed[h][k], along(second[h], k)))
            ours[h] = add_up(parts)
        ours = jnp.concatenate(ours, axis=0).astype(bf16)
        across = send(ours, pipe_from(1 - layer))
        halves = [ours, across] if layer == 0 else [across, ours]
        features = 4.0 * residual_input.shape[1]
        factor = lax.rsqrt(square / features + EPS)[:, None]
        halves = [part.astype(f32) * factor for part in halves]
        query = jnp.concatenate([part[:, :qh] for part in halves], axis=1)
        key_new = jnp.concatenate([part[:, qh : qh + kh] for part in halves], axis=1)
        value_new = jnp.concatenate([part[:, qh + kh :] for part in halves], axis=1)
        query = rotate(query.reshape(group, -1, HEAD), cosine, sine).astype(bf16)
        key_new = rotate(key_new.reshape(group, -1, HEAD), cosine, sine).astype(bf16)
        value_new = value_new.reshape(group, -1, HEAD).astype(bf16)
        attended = attend(
            query, key_new, value_new, cached_key_rows[0], cached_value_rows[0], cached_length
        )

        keep = attended[:, layer * qh : (layer + 1) * qh]
        give = attended[:, (1 - layer) * qh : (2 - layer) * qh]
        taken = send(give, pipe_from(layer))
        product = jnp.dot(attended, down, preferred_element_type=f32)
        product = product.reshape(group, ADAPTERS, RANK)
        shrunk = jnp.sum(jnp.where(chosen[:, :, None], product, 0.0), axis=1)
        shrunk = jnp.where(live, shrunk, 0.0) * rank_scale[:, None]
        shrunk = jnp.where(p == layer, shrunk, 0.0).astype(bf16)
        load = jnp.concatenate([jnp.where(p == layer, keep, taken), shrunk], axis=1)
        partial = [None, None]
        for h in range(2):
            mine = load[h * half : (h + 1) * half]
            got = [mine] + [None] * 3
            for k in (2, 1, 3):
                got[4 - k] = send(mine, along(second[h], k))
            line = jnp.concatenate(got, axis=0)
            blocks = [line] + [None] * 3
            for k in (2, 1, 3):
                blocks[4 - k] = send(line, along(first[h], k))
            out = []
            for k in range(4):
                base = jnp.dot(blocks[k][:, :qh], w_out[layer], preferred_element_type=f32)
                picked = rows_of[h][k][:, None] == slots[None, :]
                spread = jnp.where(picked[:, :, None], blocks[k][:, None, qh:], jnp.zeros((), bf16))
                spread = spread.reshape(-1, ADAPTERS * RANK)
                delta = jnp.dot(spread, up, preferred_element_type=f32)
                out.append((base + delta).astype(bf16))
            partial[h] = jnp.stack(out)

        summed = jnp.where(core == 0, partial[0], partial[1])
        summed = summed.astype(f32) + send(
            jnp.where(core == 0, partial[1], partial[0]), other_core
        ).astype(f32)
        summed = summed.astype(bf16)
        before = jnp.where(core == 0, state[0], state[1])
        if layer == 0:
            parts = [before, summed] + [send(summed, along("x", k)) for k in (2, 1, 3)]
            after = add_up(parts).astype(bf16)
            there = send(after, other_core)
            state = [jnp.where(core == 0, after, there), jnp.where(core == 0, there, after)]
        else:

            def by_distance(value):
                value = value.reshape(4, 4, half, block)
                return jnp.where(core == 0, value, value.transpose(1, 0, 2, 3))

            summed = by_distance(summed)
            parts = [
                lax.dynamic_index_in_dim(by_distance(before), x, 0, keepdims=False),
                lax.dynamic_index_in_dim(summed, x, 0, keepdims=False),
            ]
            for k in (2, 1, 3):
                piece = lax.dynamic_index_in_dim(summed, (x + k) % 4, 0, keepdims=False)
                parts.append(send(piece, along("x", k)))
            final = add_up(parts).astype(bf16)
            pieces = [None] * 4
            for k in range(4):
                pieces[(4 - k) % 4] = send(
                    final[k],
                    lambda z, y, p, u, c, k=k: (z + 2 * p + u, y + k, c, z // 2, z % 2),
                )
            pieces = jnp.stack(pieces + pieces)
            pieces = lax.dynamic_slice_in_dim(pieces, (4 - y) % 4, 4, 0)
            return pieces.transpose(1, 0, 2).reshape(half, 4 * block)


def solution(mesh):
    placed = (
        P("dp", "tensor"),
        P("pipe", None),
        P("pipe", "dp", "tensor"),
        P("pipe", "dp", "tensor"),
        P("pipe", "dp", "tensor"),
        P("pipe", "tensor", "dp"),
        P("pipe", "tensor", None, None),
        P("pipe", None, None, "tensor"),
        P("pipe", "dp", None, "tensor"),
        P("pipe", "dp", None, "tensor"),
        P("dp"),
        P(),
        P("dp"),
    )
    return jax.shard_map(
        on_device,
        mesh=mesh,
        in_specs=placed,
        out_specs=P(("dp", "pipe"), "tensor"),
        check_vma=False,
    )
```

```python
import jax
import jax.numpy as jnp
from jax import lax
from jax.experimental import pallas as pl
from jax.experimental.pallas import tpu as pltpu
from jax.sharding import Mesh
from jax.sharding import PartitionSpec as P

HEAD = 128
RANK = 128
ADAPTERS = 8
CTX = 80
EPS = 1e-05
SCALE = 64.0
LANES = 128
AXES = ("z", "y", "pipe", "xl", "core")
DP = ("z", "y")
RING = ("pipe", "xl")
bf16 = jnp.bfloat16
f32 = jnp.float32


def send(block, route):
    pairs = []
    for z in range(4):
        for y in range(4):
            for p in range(2):
                for xl in range(2):
                    for c in range(2):
                        there = route(z, y, p, xl, c)
                        if there is None:
                            continue
                        source = ((z * 4 + y) * 2 + p) * 4 + xl * 2 + c
                        a, b, q, u, v = there
                        target = (((a % 4) * 4 + b % 4) * 2 + q) * 4 + u * 2 + v
                        pairs.append((source, target))
    return lax.ppermute(block, AXES, pairs)


def other_core(z, y, p, u, c):
    return (z, y, p, u, 1 - c)


def other_xl(z, y, p, u, c):
    return (z, y, p, 1 - u, c)


def other_pipe(z, y, p, u, c):
    return (z, y, 1 - p, u, c)


def pipe_from(source):
    return lambda z, y, p, u, c: (z, y, 1 - p, u, c) if p == source else None


def exchange(blocks, axes):
    return lax.all_to_all(blocks, axes, 0, 0, tiled=True)


def after(value, earlier):
    return lax.optimization_barrier((value, earlier))[0]


def project_in_kernel(with_squares, x_ref, w_ref, out_ref):
    x = x_ref[...]
    width = w_ref.shape[1]
    out_ref[:, :width] = jnp.dot(x, w_ref[...], preferred_element_type=f32).astype(bf16)
    if with_squares:
        x = x.astype(f32)
        total = jnp.sum(x * x, axis=1, keepdims=True)
        high = total.astype(bf16).astype(f32)
        lane = lax.broadcasted_iota(jnp.int32, (x.shape[0], LANES), 1)
        out_ref[:, width:] = jnp.where(lane == 0, high, total - high).astype(bf16)


def project_in(state, weights, with_squares, tile=256):
    rows, depth = state.shape
    width = weights.shape[1]
    wide = width + LANES if with_squares else width
    return pl.pallas_call(
        lambda *refs: project_in_kernel(with_squares, *refs),
        grid=(rows // tile,),
        in_specs=[
            pl.BlockSpec((tile, depth), lambda i: (i, 0)),
            pl.BlockSpec((depth, width), lambda i: (0, 0)),
        ],
        out_specs=pl.BlockSpec((tile, wide), lambda i: (i, 0)),
        out_shape=jax.ShapeDtypeStruct((rows, wide), bf16),
        compiler_params=pltpu.CompilerParams(vmem_limit_bytes=32 * 1024 * 1024),
    )(state, weights)


def project_out_kernel(a_ref, ids_ref, w_ref, up_ref, out_ref):
    depth = w_ref.shape[0]
    total = jnp.dot(a_ref[:, :depth], w_ref[...], preferred_element_type=f32)
    shrunk = a_ref[:, depth:]
    ids = ids_ref[...]
    nothing = jnp.zeros_like(shrunk)
    spread = jnp.concatenate(
        [jnp.where(ids == a, shrunk, nothing) for a in range(ADAPTERS)], axis=1
    )
    total = total + jnp.dot(spread, up_ref[...], preferred_element_type=f32)
    out_ref[...] = total.astype(bf16)


def project_out(load, ids, weights, up, tile=256):
    rows, wide = load.shape
    depth, width = weights.shape
    return pl.pallas_call(
        project_out_kernel,
        grid=(rows // tile,),
        in_specs=[
            pl.BlockSpec((tile, wide), lambda i: (i, 0)),
            pl.BlockSpec((tile, RANK), lambda i: (i, 0)),
            pl.BlockSpec((depth, width), lambda i: (0, 0)),
            pl.BlockSpec((ADAPTERS * RANK, width), lambda i: (0, 0)),
        ],
        out_specs=pl.BlockSpec((tile, width), lambda i: (i, 0)),
        out_shape=jax.ShapeDtypeStruct((rows, width), bf16),
        compiler_params=pltpu.CompilerParams(vmem_limit_bytes=32 * 1024 * 1024),
    )(load, ids, weights, up)


def rope_tables(positions):
    half = HEAD // 2
    inv_freq = jnp.exp(-jnp.log(10000.0) * jnp.arange(half, dtype=f32) * (2.0 / HEAD))
    angles = positions.astype(f32)[:, None] * inv_freq[None, :]
    return (jnp.cos(angles), jnp.sin(angles))


def rotate(features, cosine, sine):
    half = HEAD // 2
    a = features[..., :half]
    b = features[..., half:]
    return jnp.concatenate([a * cosine - b * sine, b * cosine + a * sine], axis=-1)


def attend(query, key_new, value_new, keys, values, lengths):
    rows, groups = key_new.shape[:2]
    inverse = float(HEAD) ** (-0.5)
    query = query.reshape(rows, groups, -1, HEAD)
    keys = keys.reshape(rows, CTX, groups, HEAD)
    values = values.reshape(rows, CTX, groups, HEAD)
    scores = jnp.einsum("rgqd,rcgd->rgqc", query, keys, preferred_element_type=f32) * inverse
    own = jnp.einsum("rgqd,rgd->rgq", query, key_new, preferred_element_type=f32) * inverse
    valid = jnp.arange(CTX, dtype=jnp.int32)[None, :] < lengths[:, None]
    masked = jnp.where(valid[:, None, None, :], scores, -1e30)
    top = jnp.maximum(jnp.max(masked, axis=-1), own)
    raw = jnp.exp(masked - top[..., None])
    own_raw = jnp.exp(own - top)
    total = jnp.sum(raw, axis=-1) + own_raw
    weights = (raw / total[..., None]).astype(bf16)
    own_weight = (own_raw / total).astype(bf16)
    out = jnp.einsum("rgqc,rcgd->rgqd", weights, values, preferred_element_type=f32)
    out = out + own_weight.astype(f32)[..., None] * value_new.astype(f32)[:, :, None, :]
    return out.reshape(rows, -1).astype(bf16)


def on_device(
    residual_input,
    layer_norm_gain,
    query_weight,
    key_weight,
    value_weight,
    output_weight,
    adapter_down_weight,
    adapter_up_weight,
    cached_key_rows,
    cached_value_rows,
    request_adapter,
    rank_per_adapter,
    cached_length,
):
    z, y, p = lax.axis_index("z"), lax.axis_index("y"), lax.axis_index("pipe")
    xl, core = lax.axis_index("xl"), lax.axis_index("core")
    x = 2 * p + xl
    group = residual_input.shape[0]
    half = group // 2
    block = query_weight.shape[1]
    qh = query_weight.shape[2] // 2
    kh = key_weight.shape[2] // 2
    all_rows = 16 * group

    gain = lax.dynamic_slice_in_dim(layer_norm_gain[0], (4 * z + y) * block, block, 0)
    gain = gain.astype(f32)[:, None]

    def in_half(which):
        parts = [
            lax.dynamic_slice_in_dim(query_weight[0], which * qh, qh, 1),
            lax.dynamic_slice_in_dim(key_weight[0], which * kh, kh, 1),
            lax.dynamic_slice_in_dim(value_weight[0], which * kh, kh, 1),
        ]
        return (jnp.concatenate(parts, axis=1).astype(f32) * gain).astype(bf16)

    theirs_in = in_half(1 - p)
    cuts = (0, 176, 352, block)
    in_got = [send(theirs_in[: cuts[1]], other_pipe)]

    numbers = jnp.pad(request_adapter.astype(bf16).reshape(1, group), ((0, 15), (0, block - group)))
    got = [None] * 4
    for k in range(4):
        piece = lax.dynamic_slice_in_dim(residual_input, (y + k) % 4 * block, block, 1)
        got[(4 - k) % 4] = send(
            jnp.concatenate([piece, numbers], axis=0),
            lambda z, y, p, u, c, k=k: (2 * u + c, y + k, p, z // 2, z % 2),
        )
    got = after(got, theirs_in)
    quarter = lax.dynamic_slice_in_dim(jnp.stack(got + got), (4 - y) % 4, 4, 0)
    in_got.append(send(after(theirs_in, in_got[0])[cuts[1] : cuts[2]], other_pipe))
    near = send(after(quarter, in_got[0]), other_xl)
    pair = jnp.stack([jnp.where(xl == 0, quarter, near), jnp.where(xl == 0, near, quarter)])
    in_got.append(send(after(theirs_in, in_got[1])[cuts[2] :], other_pipe))
    far = send(after(pair, in_got[1]), other_core)
    even, odd = jnp.where(core == 0, pair, far), jnp.where(core == 0, far, pair)
    rows = jnp.stack([even[0], odd[0], even[1], odd[1]])
    in_got = jnp.concatenate(in_got, axis=0)
    state = rows[:, :, :group].reshape(all_rows, block)
    ids = rows[:, :, group, :group].reshape(all_rows, 1)
    ids = jnp.broadcast_to(ids, (all_rows, RANK))

    square = residual_input.astype(f32)
    square = jnp.sum(square * square, axis=1).reshape(1, group)
    square = square + send(square, other_xl)
    square = square + send(square, other_core)
    square = square.reshape(group, 1)

    chosen = request_adapter[:, None] == jnp.arange(ADAPTERS, dtype=jnp.int32)[None, :]
    rank = jnp.sum(jnp.where(chosen, rank_per_adapter[None, :], 0), axis=1)
    live = jnp.arange(RANK, dtype=jnp.int32)[None, :] < rank[:, None]
    rank_scale = SCALE / rank.astype(f32)
    cosine, sine = rope_tables(cached_length)
    cosine, sine = cosine[:, None, :], sine[:, None, :]

    up = adapter_up_weight[0].reshape(ADAPTERS * RANK, -1)
    up = lax.dynamic_slice_in_dim(up, y * block, block, 1)
    out_mine = lax.dynamic_slice_in_dim(output_weight[0], p * qh, qh, 0)
    out_theirs = lax.dynamic_slice_in_dim(output_weight[0], (1 - p) * qh, qh, 0)
    out_got = send(after(out_theirs, in_got), other_pipe)

    down = adapter_down_weight[0].reshape(-1, ADAPTERS * RANK)

    mine_in = in_half(p)
    for layer in range(2):
        weights = jnp.where(p == layer, mine_in, in_got)
        parts = project_in(state, weights, layer == 1)
        parts = exchange(parts.reshape(16, group, -1), DP)
        if layer == 0:
            parts, out_got = lax.optimization_barrier((parts, out_got))
            up = send(after(up, parts), lambda z, y, p, u, c: (2 * u + c, y, p, z // 2, z % 2))
        ours = jnp.sum(parts.astype(f32), axis=0)
        if layer == 1:
            square = ours[:, qh + 2 * kh : qh + 2 * kh + 1] + ours[:, qh + 2 * kh + 1 : qh + 2 * kh + 2]
        ours = ours[:, : qh + 2 * kh].astype(bf16)
        across = send(ours, pipe_from(1 - layer))
        halves = [ours, across] if layer == 0 else [across, ours]
        features = 4.0 * residual_input.shape[1]
        factor = lax.rsqrt(square / features + EPS)
        halves = [part.astype(f32) * factor for part in halves]
        query = jnp.concatenate([part[:, :qh] for part in halves], axis=1)
        key_new = jnp.concatenate([part[:, qh : qh + kh] for part in halves], axis=1)
        value_new = jnp.concatenate([part[:, qh + kh : qh + 2 * kh] for part in halves], axis=1)
        query = rotate(query.reshape(group, -1, HEAD), cosine, sine).astype(bf16)
        key_new = rotate(key_new.reshape(group, -1, HEAD), cosine, sine).astype(bf16)
        value_new = value_new.reshape(group, -1, HEAD).astype(bf16)
        attended = attend(
            query, key_new, value_new, cached_key_rows[0], cached_value_rows[0], cached_length
        )

        keep = attended[:, layer * qh : (layer + 1) * qh]
        give = attended[:, (1 - layer) * qh : (2 - layer) * qh]
        mine = jnp.where(p == layer, keep, send(give, pipe_from(layer)))
        product = jnp.dot(attended, down, preferred_element_type=f32)
        product = product.reshape(group, ADAPTERS, RANK)
        shrunk = jnp.sum(jnp.where(chosen[:, :, None], product, 0.0), axis=1)
        shrunk = jnp.where(live, shrunk, 0.0) * rank_scale[:, None]
        shrunk = jnp.where(p == layer, shrunk, 0.0)
        load = jnp.concatenate([mine, shrunk.astype(bf16)], axis=1)
        load, up = lax.optimization_barrier((load, up))
        load = exchange(jnp.broadcast_to(load[None], (16,) + load.shape), DP)
        w_out = jnp.where(p == layer, out_mine, out_got)
        partial = project_out(load.reshape(all_rows, -1), ids, w_out, up)

        if layer == 0:
            partial = partial.reshape(2, all_rows // 2, block)
            before = lax.dynamic_index_in_dim(
                state.reshape(8, all_rows // 8, block), core * 4 + x, 0, keepdims=False
            )
        else:
            partial = partial.reshape(16, 2, half, block).transpose(1, 0, 2, 3)
            before = lax.dynamic_index_in_dim(
                state.reshape(4, 4, 2, half, block), x, 0, keepdims=False
            )
            before = lax.dynamic_index_in_dim(before, core, 1, keepdims=False)
        keep = lax.dynamic_index_in_dim(partial, core, 0, keepdims=False)
        give = lax.dynamic_index_in_dim(partial, 1 - core, 0, keepdims=False)
        summed = keep.astype(f32) + send(give, other_core).astype(f32)
        summed = summed.astype(bf16).reshape(4, -1, block)
        summed = exchange(summed, RING)
        total = jnp.sum(summed.astype(f32), axis=0) + before.reshape(-1, block).astype(f32)
        total = total.astype(bf16)
        if layer == 0:
            total = exchange(jnp.broadcast_to(total[None], (4,) + total.shape), RING)
            total = total.reshape(all_rows // 2, block)
            there = send(total, other_core)
            state = jnp.concatenate(
                [jnp.where(core == 0, total, there), jnp.where(core == 0, there, total)], axis=0
            )
        else:
            total = total.reshape(4, half, block)
            pieces = [None] * 4
            for k in range(4):
                piece = lax.dynamic_index_in_dim(total, (y + k) % 4, 0, keepdims=False)
                pieces[(4 - k) % 4] = send(
                    piece, lambda z, y, p, u, c, k=k: (2 * p + u, y + k, c, z // 2, z % 2)
                )
            pieces = lax.dynamic_slice_in_dim(jnp.stack(pieces + pieces), (4 - y) % 4, 4, 0)
            return pieces.transpose(1, 0, 2).reshape(half, 4 * block)


def solution(mesh):
    torus = Mesh(mesh.devices.reshape(4, 4, 2, 2, 2), AXES)
    heads = ("xl", "core")
    placed = (
        P(DP, heads),
        P("pipe", None),
        P("pipe", DP, heads),
        P("pipe", DP, heads),
        P("pipe", DP, heads),
        P("pipe", heads, DP),
        P("pipe", heads, None, None),
        P("pipe", None, None, heads),
        P("pipe", DP, None, heads),
        P("pipe", DP, None, heads),
        P(DP),
        P(),
        P(DP),
    )
    return jax.shard_map(
        on_device,
        mesh=torus,
        in_specs=placed,
        out_specs=P(("z", "y", "pipe"), heads),
        check_vma=False,
    )
```

```python
import jax
import jax.numpy as jnp
from jax import lax
from jax.experimental import pallas as pl
from jax.experimental.pallas import tpu as pltpu
from jax.sharding import Mesh
from jax.sharding import PartitionSpec as P

HEAD = 128
RANK = 128
ADAPTERS = 8
CTX = 80
EPS = 1e-05
SCALE = 64.0
LANES = 128
PIECES = 1
AXES = ("z", "y", "pipe", "xl", "core")
DP = ("z", "y")
RING = ("pipe", "xl")
bf16 = jnp.bfloat16
f32 = jnp.float32


def send(block, route):
    pairs = []
    for z in range(4):
        for y in range(4):
            for p in range(2):
                for xl in range(2):
                    for c in range(2):
                        there = route(z, y, p, xl, c)
                        if there is None:
                            continue
                        source = ((z * 4 + y) * 2 + p) * 4 + xl * 2 + c
                        a, b, q, u, v = there
                        target = (((a % 4) * 4 + b % 4) * 2 + q) * 4 + u * 2 + v
                        pairs.append((source, target))
    return lax.ppermute(block, AXES, pairs)


def ring(step):
    def route(z, y, p, u, c):
        there = (2 * p + u + step) % 4
        return (z, y, there // 2, there % 2, c)

    return route


def other_core(z, y, p, u, c):
    return (z, y, p, u, 1 - c)


def other_xl(z, y, p, u, c):
    return (z, y, p, 1 - u, c)


def other_pipe(z, y, p, u, c):
    return (z, y, 1 - p, 1 - u, c)


def pipe_from(source):
    return lambda z, y, p, u, c: other_pipe(z, y, p, u, c) if p == source else None


def exchange(blocks, axes):
    return lax.all_to_all(blocks, axes, 0, 0, tiled=True)


def after(value, earlier):
    return lax.optimization_barrier((value, earlier))[0]


def project_in_kernel(rows, x_ref, w_ref, out_ref):
    x = x_ref[...]
    heads = w_ref.shape[1] // LANES
    result = jnp.dot(x, w_ref[...], preferred_element_type=f32).astype(bf16)
    ones = jnp.ones((16, x.shape[1]), f32)
    first = lax.broadcasted_iota(jnp.int32, (16, LANES), 0) == 0
    for i in range(out_ref.shape[0]):
        mine = slice(i * rows, (i + 1) * rows)
        for j in range(heads):
            out_ref[i, j * rows : (j + 1) * rows] = result[mine, j * LANES : (j + 1) * LANES]
        squares = x[mine].astype(f32)
        rest = jnp.zeros((LANES - rows, x.shape[1]), f32)
        squares = jnp.concatenate([squares * squares, rest], axis=0)
        total = lax.dot_general(ones, squares, (((1,), (1,)), ((), ())), preferred_element_type=f32)
        high = total.astype(bf16).astype(f32)
        out_ref[i, heads * rows :] = jnp.where(first, high, total - high).astype(bf16)


def project_in(state, weights, rows, groups=4):
    count, depth = state.shape
    width = weights.shape[1]
    length = width // LANES * rows + 16
    return pl.pallas_call(
        lambda *refs: project_in_kernel(rows, *refs),
        grid=(count // (rows * groups),),
        in_specs=[
            pl.BlockSpec((rows * groups, depth), lambda i: (i, 0)),
            pl.BlockSpec((depth, width), lambda i: (0, 0)),
        ],
        out_specs=pl.BlockSpec((groups, length, LANES), lambda i: (i, 0, 0)),
        out_shape=jax.ShapeDtypeStruct((count // rows, length, LANES), bf16),
        compiler_params=pltpu.CompilerParams(vmem_limit_bytes=32 * 1024 * 1024),
        cost_estimate=pl.CostEstimate(flops=0, bytes_accessed=0, transcendentals=0),
    )(state, weights)


def project_out_kernel(rows, _, a_ref, ids_ref, w_ref, up_ref, out_ref):
    heads = w_ref.shape[0] // LANES
    lhs, shrunk = [], []
    for i in range(a_ref.shape[0]):
        pieces = [a_ref[i, j * rows : (j + 1) * rows] for j in range(heads + 1)]
        lhs.append(jnp.concatenate(pieces[:heads], axis=1))
        shrunk.append(pieces[heads])
    lhs, shrunk = jnp.concatenate(lhs, axis=0), jnp.concatenate(shrunk, axis=0)
    total = jnp.dot(lhs, w_ref[...], preferred_element_type=f32)
    ids = ids_ref[...]
    nothing = jnp.zeros_like(shrunk)
    spread = jnp.concatenate(
        [jnp.where(ids == a, shrunk, nothing) for a in range(ADAPTERS)], axis=1
    )
    total = total + jnp.dot(spread, up_ref[...], preferred_element_type=f32)
    out_ref[...] = total.astype(bf16)


def project_out(load, ids, weights, up, rows, first, steps=2, groups=4):
    count, length, _ = load.shape
    depth, width = weights.shape
    tile = groups * rows
    return pl.pallas_call(
        lambda *refs: project_out_kernel(rows, *refs),
        grid_spec=pltpu.PrefetchScalarGridSpec(
            num_scalar_prefetch=1,
            grid=(steps,),
            in_specs=[
                pl.BlockSpec((groups, length, LANES), lambda i, f: (f[0] + i, 0, 0)),
                pl.BlockSpec((tile, RANK), lambda i, f: (f[0] + i, 0)),
                pl.BlockSpec((depth, width), lambda i, f: (0, 0)),
                pl.BlockSpec((ADAPTERS * RANK, width), lambda i, f: (0, 0)),
            ],
            out_specs=pl.BlockSpec((tile, width), lambda i, f: (i, 0)),
        ),
        out_shape=jax.ShapeDtypeStruct((steps * tile, width), bf16),
        compiler_params=pltpu.CompilerParams(vmem_limit_bytes=32 * 1024 * 1024),
        cost_estimate=pl.CostEstimate(flops=10**9, bytes_accessed=5 * 10**6, transcendentals=0),
    )(first.astype(jnp.int32).reshape(1), load, ids, weights, up)


def rope_tables(positions):
    half = HEAD // 2
    inv_freq = jnp.exp(-jnp.log(10000.0) * jnp.arange(half, dtype=f32) * (2.0 / HEAD))
    angles = positions.astype(f32)[:, None] * inv_freq[None, :]
    return (jnp.cos(angles), jnp.sin(angles))


def attention_kernel(
    g, x_ref, factor_ref, cos_ref, sin_ref, bias_ref, k_ref, v_ref, out_ref
):
    cos, sin = cos_ref[...], sin_ref[...]
    inverse = float(HEAD) ** -0.5
    x = x_ref[...].astype(f32) * factor_ref[...]
    heads = x.shape[1] // LANES - 2

    def turn(piece):
        return (piece * cos + pltpu.roll(piece, HEAD // 2, 1) * sin).astype(bf16)

    query = [turn(x[:, j * LANES : (j + 1) * LANES]) for j in range(heads)]
    key_new = turn(x[:, heads * LANES : (heads + 1) * LANES]).astype(f32)
    value_new = x[:, (heads + 1) * LANES :].astype(bf16).astype(f32)
    query = jnp.stack([q.astype(f32) for q in query], axis=1)
    keys = k_ref[:, :, g * HEAD : (g + 1) * HEAD]
    values = v_ref[:, :, g * HEAD : (g + 1) * HEAD]
    scores = jnp.einsum("rhd,rcd->rhc", query.astype(bf16), keys, preferred_element_type=f32)
    scores = scores * inverse + bias_ref[...]
    own = jnp.sum(query * key_new[:, None, :], axis=-1, keepdims=True) * inverse
    top = jnp.maximum(jnp.max(scores, axis=-1, keepdims=True), own)
    raw = jnp.exp(scores - top)
    own_raw = jnp.exp(own - top)
    total = jnp.sum(raw, axis=-1, keepdims=True) + own_raw
    weights = (raw / total).astype(bf16)
    own_weight = (own_raw / total).astype(bf16).astype(f32)
    out = jnp.einsum("rhc,rcd->rhd", weights, values, preferred_element_type=f32)
    out = out + own_weight * value_new[:, None, :]
    for j in range(heads):
        out_ref[j] = out[:, j, :].astype(bf16)


def attention(g, x, *rest):
    rows = x.shape[0]
    heads = x.shape[1] // LANES - 2
    return pl.pallas_call(
        lambda *refs: attention_kernel(g, *refs),
        in_specs=[pl.BlockSpec(memory_space=pltpu.VMEM)] * 7,
        out_specs=pl.BlockSpec(memory_space=pltpu.VMEM),
        out_shape=jax.ShapeDtypeStruct((heads, rows, HEAD), bf16),
        compiler_params=pltpu.CompilerParams(vmem_limit_bytes=40 * 1024 * 1024),
        cost_estimate=pl.CostEstimate(flops=10**9, bytes_accessed=5 * 10**6, transcendentals=0),
    )(x, *rest)


def shrink_kernel(low_ref, high_ref, down_ref, ids_ref, gate_ref, out_ref):
    flat = [ref[j] for ref in (low_ref, high_ref) for j in range(ref.shape[0])]
    product = jnp.dot(jnp.concatenate(flat, axis=1), down_ref[...], preferred_element_type=f32)
    ids = ids_ref[...]
    total = jnp.zeros(ids.shape, f32)
    for a in range(ADAPTERS):
        total = total + jnp.where(ids == a, product[:, a * RANK : (a + 1) * RANK], 0.0)
    out_ref[...] = (total * gate_ref[...]).astype(bf16)


def shrink(low, high, down, ids, gate):
    return pl.pallas_call(
        shrink_kernel,
        in_specs=[pl.BlockSpec(memory_space=pltpu.VMEM)] * 5,
        out_specs=pl.BlockSpec(memory_space=pltpu.VMEM),
        out_shape=jax.ShapeDtypeStruct(ids.shape, bf16),
        compiler_params=pltpu.CompilerParams(vmem_limit_bytes=40 * 1024 * 1024),
        cost_estimate=pl.CostEstimate(flops=10**9, bytes_accessed=5 * 10**6, transcendentals=0),
    )(low, high, down, ids, gate)


def on_device(
    residual_input,
    layer_norm_gain,
    query_weight,
    key_weight,
    value_weight,
    output_weight,
    adapter_down_weight,
    adapter_up_weight,
    cached_key_rows,
    cached_value_rows,
    request_adapter,
    rank_per_adapter,
    cached_length,
):
    z, y, p = lax.axis_index("z"), lax.axis_index("y"), lax.axis_index("pipe")
    xl, core = lax.axis_index("xl"), lax.axis_index("core")
    x = 2 * p + xl
    group = residual_input.shape[0]
    half = group // 2
    block = query_weight.shape[1]
    qh = query_weight.shape[2] // 2
    kh = key_weight.shape[2] // 2

    gain = lax.dynamic_slice_in_dim(layer_norm_gain[0], (4 * z + y) * block, block, 0)
    gain = gain.astype(f32)[:, None]

    def in_half(which):
        parts = [
            lax.dynamic_slice_in_dim(query_weight[0], which * qh, qh, 1),
            lax.dynamic_slice_in_dim(key_weight[0], which * kh, kh, 1),
            lax.dynamic_slice_in_dim(value_weight[0], which * kh, kh, 1),
        ]
        return (jnp.concatenate(parts, axis=1).astype(f32) * gain).astype(bf16)

    numbers = jnp.pad(request_adapter.astype(bf16).reshape(1, group), ((0, 15), (0, block - group)))
    turned = jnp.concatenate([residual_input, jnp.concatenate([numbers] * 4, axis=1)], axis=0)
    turned = send(turned, lambda z, y, p, u, c: (2 * u + c, y, p, z // 2, z % 2))
    theirs_in = in_half(1 - p)
    cut = block // 32 * 29
    in_first = send(theirs_in[:cut], other_pipe)
    in_rest = send(after(theirs_in, in_first)[cut:], other_pipe)
    turned = jnp.stack([turned[:, k * block : (k + 1) * block] for k in range(4)])
    quarter = exchange(turned, "y")
    near = send(quarter, other_xl)
    down = adapter_down_weight[0].reshape(-1, ADAPTERS * RANK)
    out_mine = lax.dynamic_slice_in_dim(output_weight[0], p * qh, qh, 0)
    out_theirs = lax.dynamic_slice_in_dim(output_weight[0], (1 - p) * qh, qh, 0)
    up = adapter_up_weight[0].reshape(ADAPTERS * RANK, -1)
    up = lax.dynamic_slice_in_dim(up, y * block, block, 1)
    near, down, out_theirs, up = lax.optimization_barrier((near, down, out_theirs, up))
    pair = jnp.stack([jnp.where(xl == 0, quarter, near), jnp.where(xl == 0, near, quarter)])
    far = send(pair, other_core)
    even, odd = jnp.where(core == 0, pair, far), jnp.where(core == 0, far, pair)
    rows = jnp.stack([even[0], odd[0], even[1], odd[1]])
    in_got = jnp.concatenate([in_first, in_rest], axis=0)
    size = group // PIECES
    spans = [slice(i * size, (i + 1) * size) for i in range(PIECES)]
    state = [rows[:, :, span].reshape(-1, block) for span in spans]
    ids = [rows[:, :, group, span].reshape(-1, 1) for span in spans]
    ids = [jnp.broadcast_to(part, (part.shape[0], RANK)) for part in ids]

    square = residual_input.astype(f32)
    square = jnp.sum(square * square, axis=1).reshape(1, group)
    square = square + send(square, other_xl)
    square = square + send(square, other_core)
    square = square.reshape(group, 1)

    chosen = request_adapter[:, None] == jnp.arange(ADAPTERS, dtype=jnp.int32)[None, :]
    rank = jnp.sum(jnp.where(chosen, rank_per_adapter[None, :], 0), axis=1)
    live = jnp.arange(RANK, dtype=jnp.int32)[None, :] < rank[:, None]
    rank_scale = SCALE / rank.astype(f32)
    gate = jnp.where(live, rank_scale[:, None], 0.0)
    own_ids = jnp.broadcast_to(request_adapter[:, None], (group, RANK))
    cosine, sine = rope_tables(cached_length)
    cosine = jnp.concatenate([cosine, cosine], axis=1)
    sine = jnp.concatenate([-sine, sine], axis=1)
    bias = jnp.arange(CTX, dtype=jnp.int32)[None, None, :] < cached_length[:, None, None]
    bias = jnp.where(bias, 0.0, -1e30).astype(f32)
    features = 4.0 * residual_input.shape[1]

    def later_weights(earlier):
        mine, theirs, own = after((out_mine, out_theirs, up), earlier)
        theirs = send(theirs, other_pipe)
        near = send(own, lambda z, y, p, u, c: (z, y, p, 1 - u, c) if 2 * u + c == z else None)
        own = jnp.where(2 * xl + core == z, own, near)
        far = send(own, lambda z, y, p, u, c: (z, y, p, u, 1 - c) if c == z % 2 else None)
        own = jnp.where(core == z % 2, own, far)
        return jnp.where(p == 0, mine, theirs), jnp.where(p == 1, mine, theirs), own

    def summed(layer, i, weights, previous):
        if layer == 1:
            parts = project_in(state[i], weights, size)
        else:
            parts = jnp.dot(state[i], weights, preferred_element_type=f32).astype(bf16)
            parts = parts.reshape(16, size, -1)
        parts = parts if previous is None else after(parts, previous)
        if layer == 0 and i == 0:
            w_out.extend(later_weights(parts))
        parts = exchange(parts, DP)
        if layer == 0 and i == 0:
            parts, *w_out[:] = lax.optimization_barrier((parts, *w_out))
        sums = jnp.sum(parts.astype(f32), axis=0)
        if layer == 0:
            return parts, sums.astype(bf16), square[spans[i]]
        ours = sums[:-16].reshape(-1, size, LANES).transpose(1, 0, 2).reshape(size, -1)
        squares = (sums[-16, :size] + sums[-15, :size]).reshape(size, 1)
        return parts, ours.astype(bf16), squares

    def attended(layer, i, ours, squares, previous):
        span = spans[i]
        across = send(ours, pipe_from(1 - layer))
        rest = (
            lax.rsqrt(squares / features + EPS),
            cosine[span],
            sine[span],
            bias[span],
            cached_key_rows[0, span],
            cached_value_rows[0, span],
        )
        heads = [None, None]
        heads[layer] = attention(layer, ours, *rest)
        heads[1 - layer] = attention(1 - layer, across, *rest)
        taken = send(heads[1 - layer], pipe_from(layer))
        shrunk = shrink(*heads, down, own_ids[span], jnp.where(p == layer, gate[span], 0.0))
        heads = jnp.where(p == layer, heads[layer], taken)
        load = jnp.concatenate([heads.reshape(-1, LANES), shrunk], axis=0)
        load = load if previous is None else after(load, previous)
        return load, exchange(jnp.broadcast_to(load[None], (16,) + load.shape), DP)

    def reduced(load, row_ids, weights, before):
        give = project_out(load, row_ids, weights, w_out[2], size, 2 * (1 - core))
        came = send(give, other_core).reshape(4, -1, block)
        keep = project_out(load, row_ids, weights, w_out[2], size, 2 * core)
        keep = keep.reshape(4, -1, block)
        before = before.reshape(8, -1, block)
        total = lax.dynamic_index_in_dim(before, core * 4 + x, 0, keepdims=False).astype(f32)

        def quarter_of(k):
            here = lax.dynamic_index_in_dim(keep, (x + k) % 4, 0, keepdims=False)
            there = lax.dynamic_index_in_dim(came, (x + k) % 4, 0, keepdims=False)
            return here.astype(f32) + there.astype(f32)

        parts = [send(quarter_of(k).astype(bf16), ring(k)) for k in (2, 1, 3)]
        total = total + quarter_of(0)
        for part in parts:
            total = total + part.astype(f32)
        return total.astype(bf16)

    def spread(total):
        total = exchange(jnp.broadcast_to(total[None], (4,) + total.shape), RING)
        total = total.reshape(-1, block)
        there = send(total, other_core)
        return jnp.concatenate(
            [jnp.where(core == 0, total, there), jnp.where(core == 0, there, total)], axis=0
        )

    w_out = []
    mine_in = in_half(p)
    for layer in range(2):
        weights = jnp.where(p == layer, mine_in, in_got)
        sums, loads = [], []
        got = None
        for i in range(PIECES):
            got, *found = summed(layer, i, weights, got)
            sums.append(found)
        for i in range(PIECES):
            ours, squares = sums[i]
            if i:
                ours = after(ours, load)
            load, got = attended(layer, i, ours, squares, loads[-1] if i else None)
            loads.append(got)
        state = [reduced(loads[i], ids[i], w_out[layer], state[i]) for i in range(PIECES)]
        if layer == 0:
            state = [spread(part) for part in state]

    total = state[0].reshape(4, half, block)
    pieces = []
    for m in range(4):
        other = m ^ y
        piece = lax.dynamic_index_in_dim(total, other % 2 * 2 + other // 2, 0, keepdims=False)
        pieces.append(
            send(
                piece,
                lambda z, y, p, u, c, m=m: (
                    2 * c + p,
                    2 * u + (m ^ y) % 2,
                    (m ^ y) // 2,
                    z // 2,
                    z % 2,
                ),
            )
        )
    odd = y % 2 == 1
    pieces = [jnp.where(odd, pieces[m ^ 1], pieces[m]) for m in range(4)]
    pieces = [jnp.where(p == 1, pieces[m ^ 2], pieces[m]) for m in range(4)]
    return jnp.concatenate(pieces, axis=1)


def solution(mesh):
    torus = Mesh(mesh.devices.reshape(4, 4, 2, 2, 2), AXES)
    heads = ("xl", "core")
    placed = (
        P(DP, heads),
        P("pipe", None),
        P("pipe", DP, heads),
        P("pipe", DP, heads),
        P("pipe", DP, heads),
        P("pipe", heads, DP),
        P("pipe", heads, None, None),
        P("pipe", None, None, heads),
        P("pipe", DP, None, heads),
        P("pipe", DP, None, heads),
        P(DP),
        P(),
        P(DP),
    )
    return jax.shard_map(
        on_device,
        mesh=torus,
        in_specs=placed,
        out_specs=P(("z", "y", "pipe"), heads),
        check_vma=False,
    )
```

```python
import jax
import jax.numpy as jnp
from jax import lax
from jax.experimental import pallas as pl
from jax.experimental.pallas import tpu as pltpu
from jax.sharding import Mesh
from jax.sharding import PartitionSpec as P

HEAD = 128
RANK = 128
ADAPTERS = 8
CTX = 80
EPS = 1e-05
SCALE = 64.0
LANES = 128
PIECES = 1
AXES = ("z", "y", "pipe", "xl", "core")
DP = ("z", "y")
RING = ("pipe", "xl")
bf16 = jnp.bfloat16
f32 = jnp.float32


def send(block, route):
    pairs = []
    for z in range(4):
        for y in range(4):
            for p in range(2):
                for xl in range(2):
                    for c in range(2):
                        there = route(z, y, p, xl, c)
                        if there is None:
                            continue
                        source = ((z * 4 + y) * 2 + p) * 4 + xl * 2 + c
                        a, b, q, u, v = there
                        target = (((a % 4) * 4 + b % 4) * 2 + q) * 4 + u * 2 + v
                        pairs.append((source, target))
    return lax.ppermute(block, AXES, pairs)


def ring(step):
    def route(z, y, p, u, c):
        there = (2 * p + u + step) % 4
        return (z, y, there // 2, there % 2, c)

    return route


def other_core(z, y, p, u, c):
    return (z, y, p, u, 1 - c)


def other_xl(z, y, p, u, c):
    return (z, y, p, 1 - u, c)


def other_pipe(z, y, p, u, c):
    return (z, y, 1 - p, 1 - u, c)


def pipe_from(source):
    return lambda z, y, p, u, c: other_pipe(z, y, p, u, c) if p == source else None


def exchange(blocks, axes):
    return lax.all_to_all(blocks, axes, 0, 0, tiled=True)


def after(value, earlier):
    return lax.optimization_barrier((value, earlier))[0]


def project_in_kernel(rows, x_ref, w_ref, out_ref):
    x = x_ref[...]
    heads = w_ref.shape[1] // LANES
    result = jnp.dot(x, w_ref[...], preferred_element_type=f32).astype(bf16)
    ones = jnp.ones((16, x.shape[1]), f32)
    first = lax.broadcasted_iota(jnp.int32, (16, LANES), 0) == 0
    for i in range(out_ref.shape[0]):
        mine = slice(i * rows, (i + 1) * rows)
        for j in range(heads):
            out_ref[i, j * rows : (j + 1) * rows] = result[mine, j * LANES : (j + 1) * LANES]
        squares = x[mine].astype(f32)
        rest = jnp.zeros((LANES - rows, x.shape[1]), f32)
        squares = jnp.concatenate([squares * squares, rest], axis=0)
        total = lax.dot_general(ones, squares, (((1,), (1,)), ((), ())), preferred_element_type=f32)
        high = total.astype(bf16).astype(f32)
        out_ref[i, heads * rows :] = jnp.where(first, high, total - high).astype(bf16)


def project_in(state, weights, rows, groups=4):
    count, depth = state.shape
    width = weights.shape[1]
    length = width // LANES * rows + 16
    return pl.pallas_call(
        lambda *refs: project_in_kernel(rows, *refs),
        grid=(count // (rows * groups),),
        in_specs=[
            pl.BlockSpec((rows * groups, depth), lambda i: (i, 0)),
            pl.BlockSpec((depth, width), lambda i: (0, 0)),
        ],
        out_specs=pl.BlockSpec((groups, length, LANES), lambda i: (i, 0, 0)),
        out_shape=jax.ShapeDtypeStruct((count // rows, length, LANES), bf16),
        compiler_params=pltpu.CompilerParams(vmem_limit_bytes=32 * 1024 * 1024),
        cost_estimate=pl.CostEstimate(flops=0, bytes_accessed=0, transcendentals=0),
    )(state, weights)


def project_out_kernel(rows, _, a_ref, ids_ref, w_ref, up_ref, out_ref):
    heads = w_ref.shape[0] // LANES
    lhs, shrunk = [], []
    for i in range(a_ref.shape[0]):
        pieces = [a_ref[i, j * rows : (j + 1) * rows] for j in range(heads + 1)]
        lhs.append(jnp.concatenate(pieces[:heads], axis=1))
        shrunk.append(pieces[heads])
    lhs, shrunk = jnp.concatenate(lhs, axis=0), jnp.concatenate(shrunk, axis=0)
    total = jnp.dot(lhs, w_ref[...], preferred_element_type=f32)
    ids = ids_ref[...]
    nothing = jnp.zeros_like(shrunk)
    spread = jnp.concatenate(
        [jnp.where(ids == a, shrunk, nothing) for a in range(ADAPTERS)], axis=1
    )
    total = total + jnp.dot(spread, up_ref[...], preferred_element_type=f32)
    out_ref[...] = total.astype(bf16)


def project_out(load, ids, weights, up, rows, first, megabytes, steps=2, groups=4):
    count, length, _ = load.shape
    depth, width = weights.shape
    tile = groups * rows
    return pl.pallas_call(
        lambda *refs: project_out_kernel(rows, *refs),
        grid_spec=pltpu.PrefetchScalarGridSpec(
            num_scalar_prefetch=1,
            grid=(steps,),
            in_specs=[
                pl.BlockSpec((groups, length, LANES), lambda i, f: (f[0] + i, 0, 0)),
                pl.BlockSpec((tile, RANK), lambda i, f: (f[0] + i, 0)),
                pl.BlockSpec((depth, width), lambda i, f: (0, 0)),
                pl.BlockSpec((ADAPTERS * RANK, width), lambda i, f: (0, 0)),
            ],
            out_specs=pl.BlockSpec((tile, width), lambda i, f: (i, 0)),
        ),
        out_shape=jax.ShapeDtypeStruct((steps * tile, width), bf16),
        compiler_params=pltpu.CompilerParams(vmem_limit_bytes=megabytes * 1024 * 1024),
        cost_estimate=pl.CostEstimate(flops=10**9, bytes_accessed=5 * 10**6, transcendentals=0),
    )(first.astype(jnp.int32).reshape(1), load, ids, weights, up)


def rope_tables(positions):
    half = HEAD // 2
    inv_freq = jnp.exp(-jnp.log(10000.0) * jnp.arange(half, dtype=f32) * (2.0 / HEAD))
    angles = positions.astype(f32)[:, None] * inv_freq[None, :]
    return (jnp.cos(angles), jnp.sin(angles))


def attention_kernel(
    g, x_ref, factor_ref, cos_ref, sin_ref, bias_ref, k_ref, v_ref, out_ref
):
    cos, sin = cos_ref[...], sin_ref[...]
    inverse = float(HEAD) ** -0.5
    x = x_ref[...].astype(f32) * factor_ref[...]
    heads = x.shape[1] // LANES - 2

    def turn(piece):
        return (piece * cos + pltpu.roll(piece, HEAD // 2, 1) * sin).astype(bf16)

    query = [turn(x[:, j * LANES : (j + 1) * LANES]) for j in range(heads)]
    key_new = turn(x[:, heads * LANES : (heads + 1) * LANES]).astype(f32)
    value_new = x[:, (heads + 1) * LANES :].astype(bf16).astype(f32)
    query = jnp.stack([q.astype(f32) for q in query], axis=1)
    keys = k_ref[:, :, g * HEAD : (g + 1) * HEAD]
    values = v_ref[:, :, g * HEAD : (g + 1) * HEAD]
    scores = jnp.einsum("rhd,rcd->rhc", query.astype(bf16), keys, preferred_element_type=f32)
    scores = scores * inverse + bias_ref[...]
    own = jnp.sum(query * key_new[:, None, :], axis=-1, keepdims=True) * inverse
    top = jnp.maximum(jnp.max(scores, axis=-1, keepdims=True), own)
    raw = jnp.exp(scores - top)
    own_raw = jnp.exp(own - top)
    total = jnp.sum(raw, axis=-1, keepdims=True) + own_raw
    weights = (raw / total).astype(bf16)
    own_weight = (own_raw / total).astype(bf16).astype(f32)
    out = jnp.einsum("rhc,rcd->rhd", weights, values, preferred_element_type=f32)
    out = out + own_weight * value_new[:, None, :]
    for j in range(heads):
        out_ref[j] = out[:, j, :].astype(bf16)


def attention(g, x, *rest):
    rows = x.shape[0]
    heads = x.shape[1] // LANES - 2
    return pl.pallas_call(
        lambda *refs: attention_kernel(g, *refs),
        in_specs=[pl.BlockSpec(memory_space=pltpu.VMEM)] * 7,
        out_specs=pl.BlockSpec(memory_space=pltpu.VMEM),
        out_shape=jax.ShapeDtypeStruct((heads, rows, HEAD), bf16),
        compiler_params=pltpu.CompilerParams(vmem_limit_bytes=40 * 1024 * 1024),
        cost_estimate=pl.CostEstimate(flops=10**9, bytes_accessed=5 * 10**6, transcendentals=0),
    )(x, *rest)


def shrink_kernel(g, heads_ref, down_ref, ids_ref, gate_ref, out_ref):
    flat = jnp.concatenate([heads_ref[j] for j in range(heads_ref.shape[0])], axis=1)
    depth = flat.shape[1]
    rows = slice(g * depth, (g + 1) * depth)
    product = jnp.dot(flat, down_ref[rows], preferred_element_type=f32)
    ids = ids_ref[...]
    total = jnp.zeros(ids.shape, f32)
    for a in range(ADAPTERS):
        total = total + jnp.where(ids == a, product[:, a * RANK : (a + 1) * RANK], 0.0)
    out_ref[...] = total * gate_ref[...]


def shrink(g, heads, down, ids, gate):
    return pl.pallas_call(
        lambda *refs: shrink_kernel(g, *refs),
        in_specs=[pl.BlockSpec(memory_space=pltpu.VMEM)] * 4,
        out_specs=pl.BlockSpec(memory_space=pltpu.VMEM),
        out_shape=jax.ShapeDtypeStruct(ids.shape, f32),
        compiler_params=pltpu.CompilerParams(vmem_limit_bytes=40 * 1024 * 1024),
        cost_estimate=pl.CostEstimate(flops=10**9, bytes_accessed=5 * 10**6, transcendentals=0),
    )(heads, down, ids, gate)


def on_device(
    residual_input,
    layer_norm_gain,
    query_weight,
    key_weight,
    value_weight,
    output_weight,
    adapter_down_weight,
    adapter_up_weight,
    cached_key_rows,
    cached_value_rows,
    request_adapter,
    rank_per_adapter,
    cached_length,
):
    z, y, p = lax.axis_index("z"), lax.axis_index("y"), lax.axis_index("pipe")
    xl, core = lax.axis_index("xl"), lax.axis_index("core")
    x = 2 * p + xl
    group = residual_input.shape[0]
    half = group // 2
    block = query_weight.shape[1]
    qh = query_weight.shape[2] // 2
    kh = key_weight.shape[2] // 2

    gain = lax.dynamic_slice_in_dim(layer_norm_gain[0], (4 * z + y) * block, block, 0)
    gain = gain.astype(f32)[:, None]

    def in_half(which):
        parts = [
            lax.dynamic_slice_in_dim(query_weight[0], which * qh, qh, 1),
            lax.dynamic_slice_in_dim(key_weight[0], which * kh, kh, 1),
            lax.dynamic_slice_in_dim(value_weight[0], which * kh, kh, 1),
        ]
        return (jnp.concatenate(parts, axis=1).astype(f32) * gain).astype(bf16)

    numbers = jnp.pad(request_adapter.astype(bf16).reshape(1, group), ((0, 15), (0, block - group)))
    turned = jnp.concatenate([residual_input, jnp.concatenate([numbers] * 4, axis=1)], axis=0)
    turned = send(turned, lambda z, y, p, u, c: (2 * u + c, y, p, z // 2, z % 2))
    theirs_in = in_half(1 - p)
    cut = block // 32 * 29
    in_first = send(theirs_in[:cut], other_pipe)
    in_rest = send(after(theirs_in, in_first)[cut:], other_pipe)
    turned = jnp.stack([turned[:, k * block : (k + 1) * block] for k in range(4)])
    quarter = exchange(turned, "y")
    near = send(quarter, other_xl)
    down = adapter_down_weight[0].reshape(-1, ADAPTERS * RANK)
    out_mine = lax.dynamic_slice_in_dim(output_weight[0], p * qh, qh, 0)
    out_theirs = lax.dynamic_slice_in_dim(output_weight[0], (1 - p) * qh, qh, 0)
    up = adapter_up_weight[0].reshape(ADAPTERS * RANK, -1)
    up = lax.dynamic_slice_in_dim(up, y * block, block, 1)
    near, down, out_theirs, up = lax.optimization_barrier((near, down, out_theirs, up))
    pair = jnp.stack([jnp.where(xl == 0, quarter, near), jnp.where(xl == 0, near, quarter)])
    far = send(pair, other_core)
    even, odd = jnp.where(core == 0, pair, far), jnp.where(core == 0, far, pair)
    rows = jnp.stack([even[0], odd[0], even[1], odd[1]])
    in_got = jnp.concatenate([in_first, in_rest], axis=0)
    size = group // PIECES
    spans = [slice(i * size, (i + 1) * size) for i in range(PIECES)]
    state = [rows[:, :, span].reshape(-1, block) for span in spans]
    ids = [rows[:, :, group, span].reshape(-1, 1) for span in spans]
    ids = [jnp.broadcast_to(part, (part.shape[0], RANK)) for part in ids]

    square = residual_input.astype(f32)
    square = jnp.sum(square * square, axis=1).reshape(1, group)
    square = square + send(square, other_xl)
    square = square + send(square, other_core)
    square = square.reshape(group, 1)

    chosen = request_adapter[:, None] == jnp.arange(ADAPTERS, dtype=jnp.int32)[None, :]
    rank = jnp.sum(jnp.where(chosen, rank_per_adapter[None, :], 0), axis=1)
    live = jnp.arange(RANK, dtype=jnp.int32)[None, :] < rank[:, None]
    rank_scale = SCALE / rank.astype(f32)
    gate = jnp.where(live, rank_scale[:, None], 0.0)
    own_ids = jnp.broadcast_to(request_adapter[:, None], (group, RANK))
    cosine, sine = rope_tables(cached_length)
    cosine = jnp.concatenate([cosine, cosine], axis=1)
    sine = jnp.concatenate([-sine, sine], axis=1)
    bias = jnp.arange(CTX, dtype=jnp.int32)[None, None, :] < cached_length[:, None, None]
    bias = jnp.where(bias, 0.0, -1e30).astype(f32)
    features = 4.0 * residual_input.shape[1]

    def later_weights(earlier):
        mine, theirs, own = after((out_mine, out_theirs, up), earlier)
        theirs = send(theirs, other_pipe)
        near = send(own, lambda z, y, p, u, c: (z, y, p, 1 - u, c) if 2 * u + c == z else None)
        own = jnp.where(2 * xl + core == z, own, near)
        far = send(own, lambda z, y, p, u, c: (z, y, p, u, 1 - c) if c == z % 2 else None)
        own = jnp.where(core == z % 2, own, far)
        return jnp.where(p == 0, mine, theirs), jnp.where(p == 1, mine, theirs), own

    def summed(layer, i, weights, previous):
        if layer == 1:
            parts = project_in(state[i], weights, size)
        else:
            parts = jnp.dot(state[i], weights, preferred_element_type=f32).astype(bf16)
            parts = parts.reshape(16, size, -1)
        parts = parts if previous is None else after(parts, previous)
        if layer == 0 and i == 0:
            w_out.extend(later_weights(parts))
        parts = exchange(parts, DP)
        if layer == 0 and i == 0:
            parts, ids[:], *w_out[:] = lax.optimization_barrier((parts, ids, *w_out))
        sums = jnp.sum(parts.astype(f32), axis=0)
        if layer == 0:
            return parts, sums.astype(bf16), square[spans[i]]
        ours = sums[:-16].reshape(-1, size, LANES).transpose(1, 0, 2).reshape(size, -1)
        squares = (sums[-16, :size] + sums[-15, :size]).reshape(size, 1)
        return parts, ours.astype(bf16), squares

    def attended(layer, i, ours, squares, previous):
        span = spans[i]
        across = send(ours, pipe_from(1 - layer))
        rest = (
            lax.rsqrt(squares / features + EPS),
            cosine[span],
            sine[span],
            bias[span],
            cached_key_rows[0, span],
            cached_value_rows[0, span],
        )
        heads = [None, None]
        heads[layer] = attention(layer, ours, *rest)
        scale = jnp.where(p == layer, gate[span], 0.0)
        shrunk = shrink(layer, heads[layer], down, own_ids[span], scale)
        across, heads[layer], shrunk = lax.optimization_barrier((across, heads[layer], shrunk))
        heads[1 - layer] = attention(1 - layer, across, *rest)
        taken = send(heads[1 - layer], pipe_from(layer))
        shrunk = shrunk + shrink(1 - layer, heads[1 - layer], down, own_ids[span], scale)
        heads = jnp.where(p == layer, heads[layer], taken)
        load = jnp.concatenate([heads.reshape(-1, LANES), shrunk.astype(bf16)], axis=0)
        load = load if previous is None else after(load, previous)
        return load, exchange(jnp.broadcast_to(load[None], (16,) + load.shape), DP)

    def reduced(load, row_ids, weights, before, megabytes):
        give = project_out(load, row_ids, weights, w_out[2], size, 2 * (1 - core), megabytes)
        came = send(give, other_core).reshape(4, -1, block)
        keep = project_out(load, row_ids, weights, w_out[2], size, 2 * core, megabytes)
        keep = keep.reshape(4, -1, block)
        before = before.reshape(8, -1, block)
        total = lax.dynamic_index_in_dim(before, core * 4 + x, 0, keepdims=False).astype(f32)

        def quarter_of(k):
            here = lax.dynamic_index_in_dim(keep, (x + k) % 4, 0, keepdims=False)
            there = lax.dynamic_index_in_dim(came, (x + k) % 4, 0, keepdims=False)
            return here.astype(f32) + there.astype(f32)

        parts = [send(quarter_of(k).astype(bf16), ring(k)) for k in (2, 1, 3)]
        total = total + quarter_of(0)
        for part in parts:
            total = total + part.astype(f32)
        return total.astype(bf16)

    def spread(total):
        total = exchange(jnp.broadcast_to(total[None], (4,) + total.shape), RING)
        total = total.reshape(-1, block)
        there = send(total, other_core)
        return jnp.concatenate(
            [jnp.where(core == 0, total, there), jnp.where(core == 0, there, total)], axis=0
        )

    w_out = []
    mine_in = in_half(p)
    for layer in range(2):
        weights = jnp.where(p == layer, mine_in, in_got)
        sums, loads = [], []
        got = None
        for i in range(PIECES):
            got, *found = summed(layer, i, weights, got)
            sums.append(found)
        for i in range(PIECES):
            ours, squares = sums[i]
            if i:
                ours = after(ours, load)
            load, got = attended(layer, i, ours, squares, loads[-1] if i else None)
            loads.append(got)
        room = 56 if layer == 0 else 32
        state = [reduced(loads[i], ids[i], w_out[layer], state[i], room) for i in range(PIECES)]
        if layer == 0:
            state = [spread(part) for part in state]

    total = state[0].reshape(4, half, block)
    pieces = []
    for m in range(4):
        other = m ^ y
        piece = lax.dynamic_index_in_dim(total, other % 2 * 2 + other // 2, 0, keepdims=False)
        pieces.append(
            send(
                piece,
                lambda z, y, p, u, c, m=m: (
                    2 * c + p,
                    2 * u + (m ^ y) % 2,
                    (m ^ y) // 2,
                    z // 2,
                    z % 2,
                ),
            )
        )
    odd = y % 2 == 1
    pieces = [jnp.where(odd, pieces[m ^ 1], pieces[m]) for m in range(4)]
    pieces = [jnp.where(p == 1, pieces[m ^ 2], pieces[m]) for m in range(4)]
    return jnp.concatenate(pieces, axis=1)


def solution(mesh):
    torus = Mesh(mesh.devices.reshape(4, 4, 2, 2, 2), AXES)
    heads = ("xl", "core")
    placed = (
        P(DP, heads),
        P("pipe", None),
        P("pipe", DP, heads),
        P("pipe", DP, heads),
        P("pipe", DP, heads),
        P("pipe", heads, DP),
        P("pipe", heads, None, None),
        P("pipe", None, None, heads),
        P("pipe", DP, None, heads),
        P("pipe", DP, None, heads),
        P(DP),
        P(),
        P(DP),
    )
    return jax.shard_map(
        on_device,
        mesh=torus,
        in_specs=placed,
        out_specs=P(("z", "y", "pipe"), heads),
        check_vma=False,
    )
```
